32 devices in a mesh: group: 2 (over y), tensor: 4 (over z), owner: 2 (over x), sub: 2 (over core).
Axes of the slice: x: 2, y: 2, z: 4, core: 2. Of those that a mesh axis runs over, the one named last changes fastest.
Arguments:
- activations: bfloat16 [3, 2048, 8192], P(None, 'group', 'tensor'), parts along dimension 1, may hold values from -6 to 6
- out_weight: bfloat16 [8192, 8192], P('tensor', ('owner', 'sub')), may hold values from -0.0625 to 0.0625
- shrink_base: bfloat16 [8192, 512], P('tensor'), may hold values from -0.0625 to 0.0625
- common_expand_matrix: bfloat16 [512, 8192], P('tensor', ('owner', 'sub')), may hold values from -0.25 to 0.25
- cores: bfloat16 [256, 512, 512], P(('owner', 'sub'), None, 'tensor'), may hold values from -0.25 to 0.25
- plan_ids: int32 [6, 4], P('group'), parts along dimension 0, may hold values from 0 to 255, as said below
- seg_slot: int32 [6, 8], P('group'), parts along dimension 0, may hold values from 0 to 3, as said below
- seg_length: int32 [6, 8], P('group'), parts along dimension 0, may hold values from 1 to 128, as said below
- owner_map: int32 [256], replicated, may hold values from 0 to 255, each once
Outputs:
- layer_out: bfloat16 [3, 2048, 8192], P(None, ('group', 'tensor'), ('owner', 'sub')), parts along dimension 1
The draws below stay inside these ranges and needn't reach their ends.
There are 2 independent parts, one for each index of `group`. The reference program is written for one: setup_inputs(seed, part) draws one part's arguments, and reference() takes and returns one part's arrays. A program takes and returns all parts, laid end to end along the dimension named above; an argument that names none is the same for every part. Nothing has to cross between parts.
Inputs may be any that keep to these rules, and one draw needn't show every extreme that they name: `plan_ids`: the 4 adapters of each step are distinct. `seg_slot`: every entry of a step's plan is used by at least one segment of that step. `seg_length`: each step has a segment with all 128 rows live. `owner_map`: A permutation of the slots.
All inputs are finite; a program needn't handle non-finite values.
Results may differ from the reference program's by a relative error of at most 0.0043.
Values may be sent and summed in bfloat16 or wider, within the bound.
A program may use at most 192 MiB of HBM per device.

```python
import jax
import jax.numpy as jnp

D = 8192
BASIS_RANK = 512
ADAPTERS = 256
STEPS = 3
PADDED_ROWS = 1024
SEG = 128
SEGS = 8
PLAN = 4


def draw_plan_ids(key, part):
    key = jax.random.fold_in(key, 11)
    chosen = jax.random.permutation(key, ADAPTERS)[:STEPS * PLAN]
    return chosen.reshape(STEPS, PLAN).astype(jnp.int32)


def draw_seg_slot(key, part):
    key = jax.random.fold_in(key, 23)
    rows_out = []
    for step in range(STEPS):
        first_key, second_key = jax.random.split(jax.random.fold_in(key, step))
        extra = jax.random.randint(first_key, (SEGS - PLAN,), 0, PLAN)
        listed = jnp.concatenate([jnp.arange(PLAN, dtype=jnp.int32), extra.astype(jnp.int32)])
        rows_out.append(jax.random.permutation(second_key, listed))
    return jnp.stack(rows_out).astype(jnp.int32)


def draw_seg_length(key, part):
    key = jax.random.fold_in(key, 37)
    first_key, second_key = jax.random.split(key)
    lengths = jax.random.randint(first_key, (STEPS, SEGS), 1, SEG + 1)
    where_full = jax.random.randint(second_key, (STEPS,), 0, SEGS)
    columns = jnp.arange(SEGS, dtype=jnp.int32)
    full_mask = columns[None, :] == where_full[:, None]
    return jnp.where(full_mask, SEG, lengths).astype(jnp.int32)


def strengthened(entries, stream_key, source, target, shards_of, factor):
    owner, partner = [(jnp.arange(entries.shape[position]) // (entries.shape[position] // shards_of)).reshape([-1 if axis == position else 1 for axis in range(entries.ndim)]) for position in (source, target)]
    chosen = jax.random.permutation(stream_key, shards_of)[partner]
    strong = (owner == chosen) | (owner == (partner + shards_of // 2) % shards_of)
    return jnp.where(strong, factor * entries, entries)


def block_scale(rng, extent, shards, least, largest):
    level, own = 1.0, jax.random.fold_in(rng, 6)
    for axis_at, parts in shards:
        draws = jnp.exp(jax.random.uniform(jax.random.fold_in(own, axis_at), (parts,), jnp.float32, least / len(shards), largest / len(shards)))
        level = level * jnp.repeat(draws, extent[axis_at] // parts).reshape([-1 if axis == axis_at else 1 for axis in range(len(extent))])
    return level


def centred(key, dims, width, most, cuts=(), held_as=jnp.bfloat16):
    entries = jax.random.normal(key, dims, jnp.float32) * width
    if len(cuts) > 0:
        entries = block_scale(key, dims, cuts, -0.22, 0.18) * entries
    return jnp.clip(entries, min=-most, max=most).astype(held_as)


def gaussian_with(rng, shape, width, limit, pieces, heavy, kind=jnp.bfloat16):
    values = width * jax.random.normal(rng, shape, jnp.float32)
    if pieces:
        values = values * block_scale(rng, shape, pieces, -0.22, 0.18)
    return jnp.clip(strengthened(values, jax.random.fold_in(rng, 3), *heavy), -limit, limit).astype(kind)


def setup_inputs(seed: int = 0, part: int = 0) -> dict:
    key_list = jax.random.split(jax.random.key(seed), 10)
    part_keys = jax.random.split(jax.random.fold_in(key_list[9], part), 10)
    return {
        "activations": gaussian_with(part_keys[0], (STEPS, PADDED_ROWS, D), 1.0, 6.0, ((2, 4),), (2, 1, 4, 2.0)),
        "out_weight": centred(key_list[1], (D, D), D ** -0.5, 0.0625, ((0, 4), (1, 4))),
        "shrink_base": centred(key_list[2], (D, BASIS_RANK), D ** -0.5, 0.0625, ((0, 4),)),
        "common_expand_matrix": centred(key_list[3], (BASIS_RANK, D), BASIS_RANK ** -0.5, 0.25, ((0, 4), (1, 4))),
        "cores": centred(key_list[4], (ADAPTERS, BASIS_RANK, BASIS_RANK), BASIS_RANK ** -0.5, 0.25, ((0, 4), (2, 4))),
        "plan_ids": draw_plan_ids(jax.random.fold_in(jax.random.fold_in(key_list[9], part), 71), part),
        "seg_slot": draw_seg_slot(jax.random.fold_in(jax.random.fold_in(key_list[9], part), 71), part),
        "seg_length": draw_seg_length(jax.random.fold_in(jax.random.fold_in(key_list[9], part), 71), part),
        "owner_map": jax.random.permutation(key_list[8], ADAPTERS).astype(jnp.int32),
    }


def reference(activations, out_weight, shrink_base, common_expand_matrix, cores, plan_ids, seg_slot, seg_length, owner_map):
    step_results = []
    positions = jnp.arange(SEG, dtype=jnp.int32)
    for step in range(STEPS):
        rows_in = activations[step]
        frozen_product = jnp.dot(rows_in, out_weight, preferred_element_type=jnp.float32)
        shrunk = jnp.dot(rows_in, shrink_base, preferred_element_type=jnp.float32).astype(jnp.bfloat16)
        slots = owner_map[plan_ids[step]]
        plan_cores = cores[slots]
        seg_core = plan_cores[seg_slot[step]]
        shrunk_seg = shrunk.reshape(SEGS, SEG, BASIS_RANK).astype(jnp.float32)
        adapted_output = jnp.einsum('sqr,srk->sqk', shrunk_seg, seg_core.astype(jnp.float32))
        alive_mask = positions[None, :] < seg_length[step][:, None]
        adapted_output = jnp.where(alive_mask[:, :, None], adapted_output, jnp.float32(0.0)).astype(jnp.bfloat16)
        adapter_product = jnp.dot(adapted_output.reshape(PADDED_ROWS, BASIS_RANK), common_expand_matrix, preferred_element_type=jnp.float32)
        step_results.append((frozen_product + adapter_product).astype(jnp.bfloat16))
    return jnp.stack(step_results)
```

```python
import jax
import jax.numpy as jnp
from jax import lax
from jax.sharding import PartitionSpec as P

SEG = 128


def shards(
    activations,
    out_weight,
    shrink_base,
    common_expand_matrix,
    cores,
    plan_ids,
    seg_slot,
    seg_length,
    owner_map,
):
    f32, bf16 = jnp.float32, jnp.bfloat16
    step_count, row_count, feat_local = activations.shape
    segs_n = row_count // SEG
    rank_full = shrink_base.shape[1]
    rank_local = cores.shape[2]
    column_slice = out_weight.shape[1]
    per_device = cores.shape[0]
    plan_width = plan_ids.shape[1]
    spread = lax.axis_size(("owner", "sub"))
    place = lax.axis_index(("owner", "sub"))
    flattened = activations.reshape(step_count * row_count, feat_local)

    share = rank_full // spread
    base_share = lax.dynamic_slice_in_dim(shrink_base, place * share, share, axis=1)
    partial_value = jnp.dot(flattened, base_share, preferred_element_type=f32)
    summed = lax.psum_scatter(partial_value, "tensor", scatter_dimension=0, tiled=True)
    summed = summed.astype(bf16)
    shrunk = lax.all_gather(summed, "tensor", axis=0, tiled=True)
    shrunk = lax.all_gather(shrunk, ("owner", "sub"), axis=1, tiled=True)
    shrunk = shrunk.reshape(step_count, segs_n, SEG, rank_full)

    slots = owner_map[plan_ids.reshape(-1)]
    mine = (slots // per_device) == place
    local_index = slots % per_device
    picked = [
        jnp.where(mine[k], lax.dynamic_index_in_dim(cores, local_index[k], 0, keepdims=False), 0)
        for k in range(step_count * plan_width)
    ]
    plan_cores = lax.psum(jnp.stack(picked), ("owner", "sub"))
    plan_cores = plan_cores.reshape(step_count, plan_width, rank_full, rank_local)

    positions = lax.broadcasted_iota(jnp.int32, (segs_n, SEG), 1)
    results = []
    frozen = [
        jnp.dot(activations[step], out_weight, preferred_element_type=f32)
        for step in range(step_count)
    ]
    for step in range(step_count):
        seg_core = jnp.stack(
            [
                lax.dynamic_index_in_dim(plan_cores[step], seg_slot[step, seg], 0, keepdims=False)
                for seg in range(segs_n)
            ]
        )
        adapted = jnp.einsum("sqr,srk->sqk", shrunk[step], seg_core, preferred_element_type=f32)
        alive = positions < seg_length[step][:, None]
        adapted = jnp.where(alive[:, :, None], adapted, f32(0.0)).astype(bf16)
        adapter_product = jnp.dot(
            adapted.reshape(row_count, rank_local),
            common_expand_matrix,
            preferred_element_type=f32,
        )
        total = (frozen[step] + adapter_product).astype(bf16)
        results.append(lax.psum_scatter(total, "tensor", scatter_dimension=0, tiled=True))
    return jnp.stack(results)


def solution(mesh):
    return jax.shard_map(
        shards,
        mesh=mesh,
        in_specs=(
            P(None, "group", "tensor"),
            P("tensor", ("owner", "sub")),
            P("tensor", None),
            P("tensor", ("owner", "sub")),
            P(("owner", "sub"), None, "tensor"),
            P("group", None),
            P("group", None),
            P("group", None),
            P(),
        ),
        out_specs=P(None, ("group", "tensor"), ("owner", "sub")),
        check_vma=False,
    )
```

```python
import jax
import jax.numpy as jnp
from jax import lax
from jax.sharding import PartitionSpec as P

SEG = 128


def shards(
    activations,
    out_weight,
    shrink_base,
    common_expand_matrix,
    cores,
    plan_ids,
    seg_slot,
    seg_length,
    owner_map,
):
    f32, bf16 = jnp.float32, jnp.bfloat16
    step_count, row_count, feat_local = activations.shape
    segs_n = row_count // SEG
    rank_full = shrink_base.shape[1]
    rank_local = cores.shape[2]
    column_slice = out_weight.shape[1]
    per_device = cores.shape[0]
    plan_width = plan_ids.shape[1]
    spread = lax.axis_size(("owner", "sub"))
    place = lax.axis_index(("owner", "sub"))
    share = rank_full // spread
    base_share = lax.dynamic_slice_in_dim(shrink_base, place * share, share, axis=1)

    def shrink_partial(steps, base):
        return jnp.dot(
            steps.reshape(steps.shape[0] * row_count, feat_local), base, preferred_element_type=f32
        )

    def shrink_finish(partial_value):
        summed = lax.psum_scatter(partial_value, "tensor", scatter_dimension=0, tiled=True)
        pieces = lax.all_gather(summed.astype(bf16), ("tensor", "owner", "sub"), axis=0)
        rows = pieces.shape[1]
        pieces = pieces.reshape(-1, spread, rows, share).transpose(0, 2, 1, 3)
        return pieces.reshape(-1, row_count, rank_full)

    first, rest = activations[:1], activations[1:]
    partial_first = shrink_partial(first, base_share)

    partial_first, wanted = lax.optimization_barrier((partial_first, plan_ids.reshape(-1)))
    slots = owner_map[wanted]
    mine = (slots // per_device) == place
    picked = jnp.where(mine[:, None, None], cores[slots % per_device], bf16(0))
    picked, base_later = lax.optimization_barrier((picked, base_share))
    plan_cores = lax.psum(picked, ("owner", "sub"))
    plan_cores = plan_cores.reshape(step_count, plan_width, rank_full, rank_local)
    shrunk_first = shrink_finish(partial_first)
    shrunk_rest = shrink_finish(shrink_partial(rest, base_later))

    positions = lax.broadcasted_iota(jnp.int32, (segs_n, SEG), 1)

    def adapt(step, shrunk):
        each = jnp.einsum(
            "qr,prk->pqk", shrunk, plan_cores[step], preferred_element_type=f32
        ).reshape(plan_width, segs_n, SEG, rank_local)
        alive = positions < seg_length[step][:, None]
        adapted = jnp.zeros((segs_n, SEG, rank_local), f32)
        for entry in range(plan_width):
            chosen = alive & (seg_slot[step] == entry)[:, None]
            adapted = jnp.where(chosen[:, :, None], each[entry], adapted)
        return adapted.astype(bf16).reshape(row_count, rank_local)

    def scatter(total):
        return lax.psum_scatter(total.astype(bf16), "tensor", scatter_dimension=1, tiled=True)

    def freeze(steps):
        return jnp.einsum("sqf,fc->sqc", steps, out_weight, preferred_element_type=f32)

    def expand(adapted):
        return jnp.einsum("sqk,kc->sqc", adapted, common_expand_matrix, preferred_element_type=f32)

    frozen_first = lax.optimization_barrier(freeze(first))
    out_first = scatter(frozen_first + expand(adapt(0, shrunk_first[0])[None]))
    adapted_rest = jnp.stack([adapt(step, shrunk_rest[step - 1]) for step in range(1, step_count)])
    out_rest = scatter(freeze(rest) + expand(adapted_rest))
    return jnp.concatenate([out_first, out_rest])


def solution(mesh):
    return jax.shard_map(
        shards,
        mesh=mesh,
        in_specs=(
            P(None, "group", "tensor"),
            P("tensor", ("owner", "sub")),
            P("tensor", None),
            P("tensor", ("owner", "sub")),
            P(("owner", "sub"), None, "tensor"),
            P("group", None),
            P("group", None),
            P("group", None),
            P(),
        ),
        out_specs=P(None, ("group", "tensor"), ("owner", "sub")),
        check_vma=False,
    )
```

```python
import jax
import jax.numpy as jnp
from jax import lax
from jax.experimental.layout import Layout, with_layout_constraint
from jax.sharding import PartitionSpec as P

SEG = 128


def shards(
    activations,
    out_weight,
    shrink_base,
    common_expand_matrix,
    cores,
    plan_ids,
    seg_slot,
    seg_length,
    owner_map,
):
    f32, bf16 = jnp.float32, jnp.bfloat16
    step_count, row_count, feat_local = activations.shape
    segs_n = row_count // SEG
    rank_full = shrink_base.shape[1]
    rank_local = cores.shape[2]
    column_slice = out_weight.shape[1]
    per_device = cores.shape[0]
    plan_width = plan_ids.shape[1]
    spread = lax.axis_size(("owner", "sub"))
    place = lax.axis_index(("owner", "sub"))
    own_segs = segs_n // spread
    own_rows = own_segs * SEG
    own = lax.dynamic_slice_in_dim(activations, place * own_rows, own_rows, axis=1)
    partial_value = jnp.dot(
        own.reshape(step_count * own_rows, feat_local), shrink_base, preferred_element_type=f32
    )

    partial_value, wanted = lax.optimization_barrier((partial_value, plan_ids.reshape(-1)))
    slots = owner_map[wanted]
    mine = (slots // per_device) == place
    picked = jnp.where(mine[:, None, None], cores[slots % per_device], bf16(0))
    picked, weight = lax.optimization_barrier((picked, out_weight))
    plan_cores = lax.psum(picked, ("owner", "sub"))
    plan_cores = plan_cores.reshape(step_count, plan_width, rank_full, rank_local)

    summed = lax.psum_scatter(partial_value, "tensor", scatter_dimension=0, tiled=True)
    shrunk = lax.all_gather(summed.astype(bf16), "tensor", axis=0, tiled=True)
    shrunk = shrunk.reshape(step_count, own_rows, rank_full)
    each = jnp.einsum("sqr,sprk->spqk", shrunk, plan_cores, preferred_element_type=f32)
    each = each.reshape(step_count, plan_width, own_segs, SEG, rank_local)
    own_slot = lax.dynamic_slice_in_dim(seg_slot, place * own_segs, own_segs, axis=1)
    own_length = lax.dynamic_slice_in_dim(seg_length, place * own_segs, own_segs, axis=1)
    positions = lax.broadcasted_iota(jnp.int32, (step_count, own_segs, SEG), 2)
    alive = positions < own_length[:, :, None]
    adapted = jnp.zeros((step_count, own_segs, SEG, rank_local), f32)
    for entry in range(plan_width):
        chosen = alive & (own_slot == entry)[:, :, None]
        adapted = jnp.where(chosen[..., None], each[:, entry], adapted)
    adapted = adapted.astype(bf16).reshape(step_count * own_rows, rank_local)
    adapted = lax.all_gather(adapted, ("owner", "sub"), axis=0)
    adapted = adapted.reshape(spread, step_count, own_rows, rank_local).transpose(1, 0, 2, 3)
    adapted = adapted.reshape(step_count, row_count, rank_local)

    def scatter(total):
        return lax.psum_scatter(total.astype(bf16), "tensor", scatter_dimension=1, tiled=True)

    def freeze(steps):
        rows = steps.reshape(-1, feat_local)
        return jnp.dot(rows, weight, preferred_element_type=f32).reshape(*steps.shape[:2], -1)

    def expand(rows):
        flat = rows.reshape(-1, rank_local)
        flat = jnp.dot(flat, common_expand_matrix, preferred_element_type=f32)
        return flat.reshape(*rows.shape[:2], -1)

    frozen_first = jnp.dot(activations[0], weight, preferred_element_type=f32)
    frozen_first = with_layout_constraint(frozen_first, Layout(major_to_minor=(0, 1)))
    frozen_first = lax.optimization_barrier(frozen_first)
    extra_first = jnp.dot(adapted[0], common_expand_matrix, preferred_element_type=f32)
    total_first = (frozen_first + extra_first).astype(bf16)
    total_first = with_layout_constraint(total_first, Layout(major_to_minor=(0, 1)))
    out_first = lax.psum_scatter(total_first, "tensor", scatter_dimension=0, tiled=True)[None]
    out_rest = scatter(freeze(activations[1:]) + expand(adapted[1:]))
    return jnp.concatenate([out_first, out_rest])


def solution(mesh):
    return jax.shard_map(
        shards,
        mesh=mesh,
        in_specs=(
            P(None, "group", "tensor"),
            P("tensor", ("owner", "sub")),
            P("tensor", None),
            P("tensor", ("owner", "sub")),
            P(("owner", "sub"), None, "tensor"),
            P("group", None),
            P("group", None),
            P("group", None),
            P(),
        ),
        out_specs=P(None, ("group", "tensor"), ("owner", "sub")),
        check_vma=False,
    )
```

```python
import jax
import jax.numpy as jnp
from jax import lax
from jax.experimental.layout import Layout, with_layout_constraint
from jax.sharding import PartitionSpec as P

SEG = 128


def shards(
    activations,
    out_weight,
    shrink_base,
    common_expand_matrix,
    cores,
    plan_ids,
    seg_slot,
    seg_length,
    owner_map,
):
    f32, bf16 = jnp.float32, jnp.bfloat16
    step_count, row_count, feat_local = activations.shape
    segs_n = row_count // SEG
    rank_full = shrink_base.shape[1]
    rank_local = cores.shape[2]
    column_slice = out_weight.shape[1]
    per_device = cores.shape[0]
    plan_width = plan_ids.shape[1]
    spread = lax.axis_size(("owner", "sub"))
    place = lax.axis_index(("owner", "sub"))
    own_segs = segs_n // spread
    own_rows = own_segs * SEG
    own = lax.dynamic_slice_in_dim(activations, place * own_rows, own_rows, axis=1)
    partial_value = jnp.dot(
        own.reshape(step_count * own_rows, feat_local), shrink_base, preferred_element_type=f32
    )

    partial_value, wanted = lax.optimization_barrier((partial_value, plan_ids.reshape(-1)))
    slots = owner_map[wanted]
    mine = (slots // per_device) == place
    picked = jnp.where(mine[:, None, None], cores[slots % per_device], bf16(0))
    picked, weight = lax.optimization_barrier((picked, out_weight))
    plan_cores = lax.psum(picked, ("owner", "sub"))
    plan_cores = plan_cores.reshape(step_count, plan_width, rank_full, rank_local)

    summed = lax.psum_scatter(partial_value, "tensor", scatter_dimension=0, tiled=True)
    shrunk = lax.all_gather(summed.astype(bf16), "tensor", axis=0, tiled=True)
    shrunk = shrunk.reshape(step_count, own_rows, rank_full)
    each = jnp.einsum("sqr,sprk->spqk", shrunk, plan_cores, preferred_element_type=f32)
    each = each.reshape(step_count, plan_width, own_segs, SEG, rank_local)
    own_slot = lax.dynamic_slice_in_dim(seg_slot, place * own_segs, own_segs, axis=1)
    own_length = lax.dynamic_slice_in_dim(seg_length, place * own_segs, own_segs, axis=1)
    positions = lax.broadcasted_iota(jnp.int32, (step_count, own_segs, SEG), 2)
    alive = positions < own_length[:, :, None]
    adapted = jnp.zeros((step_count, own_segs, SEG, rank_local), f32)
    for entry in range(plan_width):
        chosen = alive & (own_slot == entry)[:, :, None]
        adapted = jnp.where(chosen[..., None], each[:, entry], adapted)
    adapted = adapted.astype(bf16).reshape(step_count, own_rows, rank_local)

    def gather(part):
        everyones = lax.all_gather(part, ("owner", "sub"), axis=0)
        return everyones.transpose(1, 0, 2, 3).reshape(part.shape[0], row_count, rank_local)

    adapted_first, adapted_rest = gather(adapted[:1]), adapted[1:]

    def scatter(total):
        return lax.psum_scatter(total.astype(bf16), "tensor", scatter_dimension=1, tiled=True)

    def freeze(steps):
        rows = steps.reshape(-1, feat_local)
        return jnp.dot(rows, weight, preferred_element_type=f32).reshape(*steps.shape[:2], -1)

    def expand(rows):
        flat = rows.reshape(-1, rank_local)
        flat = jnp.dot(flat, common_expand_matrix, preferred_element_type=f32)
        return flat.reshape(*rows.shape[:2], -1)

    frozen_first = jnp.dot(activations[0], weight, preferred_element_type=f32)
    frozen_first = with_layout_constraint(frozen_first, Layout(major_to_minor=(0, 1)))
    frozen_first = lax.optimization_barrier(frozen_first)
    extra_first = jnp.dot(adapted_first[0], common_expand_matrix, preferred_element_type=f32)
    total_first = (frozen_first + extra_first).astype(bf16)
    total_first = with_layout_constraint(total_first, Layout(major_to_minor=(0, 1)))
    out_first = lax.psum_scatter(total_first, "tensor", scatter_dimension=0, tiled=True)[None]
    _, adapted_rest = lax.optimization_barrier((total_first, adapted_rest))
    out_rest = scatter(freeze(activations[1:]) + expand(gather(adapted_rest)))
    return jnp.concatenate([out_first, out_rest])


def solution(mesh):
    return jax.shard_map(
        shards,
        mesh=mesh,
        in_specs=(
            P(None, "group", "tensor"),
            P("tensor", ("owner", "sub")),
            P("tensor", None),
            P("tensor", ("owner", "sub")),
            P(("owner", "sub"), None, "tensor"),
            P("group", None),
            P("group", None),
            P("group", None),
            P(),
        ),
        out_specs=P(None, ("group", "tensor"), ("owner", "sub")),
        check_vma=False,
    )
```
